1024 devices in a mesh: lat: 64 (over x, z), agg: 16 (over y, core).
Axes of the slice: x: 8, y: 8, z: 8, core: 2. Of those that a mesh axis runs over, the one named last changes fastest.
Arguments:
- solution: float32 [12, 256, 64, 128], P(None, 'lat', 'agg'), may hold values from -6 to 6
- right_side: float32 [12, 256, 64, 128], P(None, 'lat', 'agg'), may hold values from -6 to 6
- links: bfloat16 [4, 3, 3, 256, 64, 128], P(None, None, None, 'lat', 'agg'), may hold values from -3.5 to 3.5
- clover: bfloat16 [2, 6, 6, 256, 64, 128], P(None, None, None, 'lat', 'agg'), may hold values from -2.5 to 2.5
- null_vectors: bfloat16 [48, 12, 256, 64, 128], P(None, None, 'lat', 'agg'), may hold values from -0.109375 to 0.109375
- coarse_inverse: bfloat16 [64, 16, 8, 48, 48], P('lat', 'agg'), may hold values from -0.875 to 0.875
- coarse_links: bfloat16 [8, 64, 16, 8, 48, 48], P(None, 'lat', 'agg'), may hold values from -0.15625 to 0.15625
Outputs:
- updated: float32 [12, 256, 64, 128], P(None, 'lat', 'agg')
- residual_after: float32 [12, 256, 64, 128], P(None, 'lat', 'agg')
The draws below stay inside these ranges and needn't reach their ends.
All inputs are finite; a program needn't handle non-finite values.
Results may differ from the reference program's by a relative error of at most 0.0075.
Values sent between devices are 32-bit elements; how exact they have to be, the bound alone decides.
No kernel may reach another device: no remote copies, remote signals or barrier semaphores. Data moves between devices by JAX's collectives and lax.ppermute only.
A program may use at most 32 MiB of HBM per device.

```python
import jax
import jax.numpy as jnp
import numpy as np
from jax import lax

CY = 8
CZ = 16
NV = 48
SWEEPS = 2
NT = 256
NX = 64
YZ = 128
NTC = 64
NXC = 16
YZC = 8


def level_of(key, extent, split, low, high):
    level = 1.0
    for axis_at, parts in split:
        steps = jax.random.uniform(jax.random.fold_in(jax.random.fold_in(key, 6), axis_at), (parts,), jnp.float32, low / len(split), high / len(split))
        level = level * jnp.repeat(jnp.exp(steps), extent[axis_at] // parts).reshape((-1,) + (1,) * (len(extent) - 1 - axis_at))
    return level


def normal_values(stream_key, dims, spread, most, pieces=(), kind=jnp.bfloat16):
    drawn = spread * jax.random.normal(stream_key, dims, jnp.float32)
    if pieces:
        drawn = drawn * level_of(stream_key, dims, pieces, -0.22, 0.18)
    return jnp.clip(drawn, -most, most).astype(kind)


def setup_inputs(seed: int = 0) -> dict:
    key_list = jax.random.split(jax.random.key(seed), 8)
    return {
        "solution": normal_values(key_list[0], (12, NT, NX, YZ), 1.0, 6.0, ((1, 64), (2, 16)), jnp.float32),
        "right_side": normal_values(key_list[1], (12, NT, NX, YZ), 1.0, 6.0, ((1, 64), (2, 16)), jnp.float32),
        "links": normal_values(key_list[2], (4, 3, 3, NT, NX, YZ), 3 ** -0.5, 3.5, ((3, 64), (4, 16))),
        "clover": normal_values(key_list[3], (2, 6, 6, NT, NX, YZ), 6 ** -0.5, 2.5, ((3, 64), (4, 16))),
        "null_vectors": normal_values(key_list[4], (NV, 12, NT, NX, YZ), (12 * 256) ** -0.5, 0.109375, ((2, 64), (3, 16))),
        "coarse_inverse": normal_values(key_list[5], (NTC, NXC, YZC, NV, NV), NV ** -0.5, 0.875, ((0, 64), (1, 16))),
        "coarse_links": normal_values(key_list[6], (8, NTC, NXC, YZC, NV, NV), (32 * NV) ** -0.5, 0.15625, ((1, 64), (2, 16))),
    }


exact_mode = lax.Precision.HIGHEST
hopping = 0.5
wilson_mass = 4.0


def gamma_table():
    table = np.zeros((4, 4, 4), np.float32)
    table[0] = [[0, 0, 1, 0], [0, 0, 0, 1], [1, 0, 0, 0], [0, 1, 0, 0]]
    table[1] = [[0, 0, 0, 1], [0, 0, 1, 0], [0, 1, 0, 0], [1, 0, 0, 0]]
    table[2] = [[1, 0, 0, 0], [0, 1, 0, 0], [0, 0, -1, 0], [0, 0, 0, -1]]
    table[3] = [[0, 1, 0, 0], [1, 0, 0, 0], [0, 0, 0, -1], [0, 0, -1, 0]]
    return table


def spin_apply(matrix, spinor):
    return jnp.einsum("st,t...->s...", jnp.asarray(matrix, spinor.dtype), spinor, precision=exact_mode)


def color_apply(transport, spinor):
    total = transport[None, :, 0] * spinor[:, None, 0]
    for inner in range(1, 3):
        total = total + transport[None, :, inner] * spinor[:, None, inner]
    return total


def dirac(field, links, clover):
    depth, width = field.shape[1], field.shape[2]
    shape6 = (4, 3, depth, width, CY, CZ)
    spinor = field.reshape(shape6)
    transport = links.astype(field.dtype).reshape((4, 3, 3, depth, width, CY, CZ))
    halves = field.reshape((2, 6, depth, width, CY, CZ))
    blocks = clover.astype(field.dtype).reshape((2, 6, 6, depth, width, CY, CZ))
    local = blocks[:, :, 0] * halves[:, None, 0]
    for inner in range(1, 6):
        local = local + blocks[:, :, inner] * halves[:, None, inner]
    gammas = gamma_table()
    identity = np.eye(4, dtype=np.float32)
    hops = jnp.zeros(shape6, field.dtype)
    for axis in range(4):
        ahead = jnp.roll(spinor, -1, axis=2 + axis)
        forward = color_apply(transport[axis], spin_apply(identity - gammas[axis], ahead))
        moved = color_apply(jnp.swapaxes(transport[axis], 0, 1), spinor)
        backward = spin_apply(identity + gammas[axis], jnp.roll(moved, 1, axis=2 + axis))
        hops = hops + forward + backward
    total = wilson_mass * spinor + local.reshape(shape6) - hopping * hops
    return total.reshape(field.shape)


def restrict(rough, null_vectors):
    count = rough.shape[1] // 4
    width = rough.shape[2]

    def one_slab(index):
        start = (index * 4).astype(jnp.int32)
        piece = lax.dynamic_slice_in_dim(rough, start, 4, 1).astype(jnp.float32)
        vecs = lax.dynamic_slice_in_dim(null_vectors, start, 4, 2).astype(jnp.float32)
        piece = piece.reshape(12, 4, width // 4, 4, CY // 4, 4, CZ // 4, 4)
        vecs = vecs.reshape(NV, 12, 4, width // 4, 4, CY // 4, 4, CZ // 4, 4)
        coarse = jnp.einsum("kmaqbrcsd,maqbrcsd->qrsk", vecs, piece, precision=exact_mode)
        return coarse.reshape(width // 4, (CY // 4) * (CZ // 4), NV)

    return lax.map(one_slab, jnp.arange(count, dtype=jnp.int32))


def prolong(coarse_rounded, null_vectors):
    count = coarse_rounded.shape[0]
    width = null_vectors.shape[3]

    def one_slab(index):
        start = (index * 4).astype(jnp.int32)
        vecs = lax.dynamic_slice_in_dim(null_vectors, start, 4, 2).astype(jnp.float32)
        vecs = vecs.reshape(NV, 12, 4, width // 4, 4, CY // 4, 4, CZ // 4, 4)
        part = lax.dynamic_index_in_dim(coarse_rounded, index.astype(jnp.int32), 0, keepdims=False)
        part = part.astype(jnp.float32).reshape(width // 4, CY // 4, CZ // 4, NV)
        fine = jnp.einsum("kmaqbrcsd,qrsk->maqbrcsd", vecs, part, precision=exact_mode)
        return fine.reshape(12, 4, width, CY * CZ)

    slabs = lax.map(one_slab, jnp.arange(count, dtype=jnp.int32))
    return jnp.moveaxis(slabs, 0, 1).reshape(12, count * 4, width, CY * CZ)


def coarse_neighbours(approx):
    grid = approx.reshape(approx.shape[0], approx.shape[1], CY // 4, CZ // 4, approx.shape[3])
    found = []
    for axis in range(4):
        found.append(jnp.roll(grid, -1, axis).reshape(approx.shape))
        found.append(jnp.roll(grid, 1, axis).reshape(approx.shape))
    return jnp.stack(found)


def coarse_sweep(approx, coarse_rhs, inverse, couplings):
    near = coarse_neighbours(approx)
    off_terms = jnp.einsum("dpqskl,dpqsl->pqsk", couplings, near, precision=exact_mode)
    return jnp.einsum("pqskl,pqsl->pqsk", inverse, coarse_rhs - off_terms, precision=exact_mode)


def reference(solution, right_side, links, clover, null_vectors, coarse_inverse, coarse_links):
    residual = right_side - dirac(solution, links, clover)
    rough = residual.astype(jnp.bfloat16)
    coarse_rhs = restrict(rough, null_vectors)
    inverse = coarse_inverse.astype(jnp.float32)
    couplings = coarse_links.astype(jnp.float32)
    approx = jnp.einsum("pqskl,pqsl->pqsk", inverse, coarse_rhs, precision=exact_mode)
    for sweep in range(SWEEPS):
        approx = coarse_sweep(approx, coarse_rhs, inverse, couplings)
    correction = prolong(approx.astype(jnp.bfloat16), null_vectors)
    updated = solution + correction
    return updated, right_side - dirac(updated, links, clover)
```

```python
import jax
import jax.numpy as jnp
from jax import lax
from jax.experimental import pallas as pl
from jax.experimental.pallas import tpu as pltpu
from jax.sharding import PartitionSpec as P

CY = 8
CZ = 16
SWEEPS = 2
ROWS = 16
LANES = 128
FACE = 4
SPAN = 4

exact_mode = lax.Precision.HIGHEST
hopping = 0.5
wilson_mass = 4.0

VMEM = pl.BlockSpec(memory_space=pltpu.VMEM)
LIMIT = 24 * 1024 * 1024

EXPAND = {
    (0, 1): ((0, 0, 1), (1, 1, 1), (2, 0, -1), (3, 1, -1)),
    (0, -1): ((0, 0, 1), (1, 1, 1), (2, 0, 1), (3, 1, 1)),
    (1, 1): ((0, 0, 1), (3, 0, -1), (1, 1, 1), (2, 1, -1)),
    (1, -1): ((0, 0, 1), (3, 0, 1), (1, 1, 1), (2, 1, 1)),
    (2, 1): ((2, 0, 1), (3, 1, 1)),
    (2, -1): ((0, 0, 1), (1, 1, 1)),
    (3, 1): ((0, 0, 1), (1, 0, -1), (2, 1, 1), (3, 1, 1)),
    (3, -1): ((0, 0, 1), (1, 0, 1), (2, 1, 1), (3, 1, -1)),
}


def half(v, axis, direction):
    def mix(a, b, sign):
        return [v[a * 3 + c] + v[b * 3 + c] if sign > 0 else v[a * 3 + c] - v[b * 3 + c] for c in range(3)]

    if axis == 0:
        return mix(0, 2, -direction) + mix(1, 3, -direction)
    if axis == 1:
        return mix(0, 3, -direction) + mix(1, 2, -direction)
    if axis == 2:
        first = 2 if direction == 1 else 0
        return [2.0 * v[first * 3 + c] for c in range(6)]
    return mix(0, 1, -direction) + mix(2, 3, direction)


def transport(links_ref, axis, h, transposed):
    found = [None] * 6
    for i in range(3):
        for j in range(3):
            u = links_ref[axis * 9 + (j * 3 + i if transposed else i * 3 + j)].astype(jnp.float32)
            for spin in range(2):
                term = u * h[spin * 3 + j]
                at = spin * 3 + i
                found[at] = term if found[at] is None else found[at] + term
    return found


def place(dim):
    return lax.broadcasted_iota(jnp.int32, (ROWS, LANES), dim)


def shifted(value, axis, direction, halo):
    if axis == 0:
        moved = pltpu.roll(value, (-direction * FACE) % ROWS, 0)
        edge = ROWS // FACE - 1 if direction == 1 else 0
        return jnp.where(place(0) // FACE == edge, halo, moved)
    if axis == 1:
        moved = pltpu.roll(value, (-direction) % ROWS, 0)
        edge = FACE - 1 if direction == 1 else 0
        return jnp.where(place(0) % FACE == edge, halo, moved)
    if axis == 2:
        return pltpu.roll(value, (-direction * CZ) % LANES, 1)
    inside = pltpu.roll(value, (-direction) % LANES, 1)
    wrapped = pltpu.roll(value, (direction * (CZ - 1)) % LANES, 1)
    edge = CZ - 1 if direction == 1 else 0
    return jnp.where(place(1) % CZ == edge, wrapped, inside)


def halo_tile(halo_ref, axis, c):
    face = halo_ref[c * FACE : (c + 1) * FACE, :]
    if axis == 0:
        return jnp.concatenate([face] * (ROWS // FACE), axis=0)
    tile = jnp.broadcast_to(face[0:1], (ROWS, LANES))
    for t in range(1, FACE):
        tile = jnp.where(place(0) // FACE == t, jnp.broadcast_to(face[t : t + 1], (ROWS, LANES)), tile)
    return tile


def dirac(v, links_ref, clover_ref, halos):
    hops = [None] * 12
    for axis in range(4):
        for direction in (1, -1):
            h = half(v, axis, direction)
            if direction == -1:
                h = transport(links_ref, axis, h, True)
            near = []
            for c in range(6):
                halo = halo_tile(halos[axis, direction], axis, c) if axis < 2 else None
                near.append(shifted(h[c], axis, direction, halo))
            if direction == 1:
                near = transport(links_ref, axis, near, False)
            for spin, part, sign in EXPAND[axis, direction]:
                for c in range(3):
                    at, term = spin * 3 + c, near[part * 3 + c]
                    if hops[at] is None:
                        hops[at] = term if sign > 0 else -term
                    else:
                        hops[at] = hops[at] + term if sign > 0 else hops[at] - term
    total = []
    for block in range(2):
        for i in range(6):
            local = None
            for j in range(6):
                term = clover_ref[(block * 6 + i) * 6 + j].astype(jnp.float32) * v[block * 6 + j]
                local = term if local is None else local + term
            at = block * 6 + i
            total.append(wilson_mass * v[at] + local - hopping * hops[at])
    return total


def write_faces(v, links_ref, faces, work_ref):
    t_up, t_down, x_up, x_down = faces
    back = transport(links_ref, 0, half(v, 0, -1), True)
    ahead = half(v, 0, 1)
    for c in range(6):
        t_up[c * FACE : (c + 1) * FACE, :] = back[c][ROWS - FACE :]
        t_down[c * FACE : (c + 1) * FACE, :] = ahead[c][:FACE]
    back = transport(links_ref, 1, half(v, 1, -1), True)
    ahead = half(v, 1, 1)
    for c in range(6):
        work_ref[c] = back[c]
        work_ref[6 + c] = ahead[c]
    for c in range(6):
        x_up[c * FACE : (c + 1) * FACE, :] = work_ref[c, pl.ds(FACE - 1, FACE, stride=FACE), :]
        x_down[c * FACE : (c + 1) * FACE, :] = work_ref[6 + c, pl.ds(0, FACE, stride=FACE), :]


def faces_kernel(field_ref, links_ref, t_up, t_down, x_up, x_down, work_ref):
    write_faces([field_ref[m] for m in range(12)], links_ref, (t_up, t_down, x_up, x_down), work_ref)


def residual_tiles(field_ref, right_ref, links_ref, clover_ref, t_back, t_ahead, x_back, x_ahead):
    halos = {(0, -1): t_back, (0, 1): t_ahead, (1, -1): x_back, (1, 1): x_ahead}
    total = dirac([field_ref[m] for m in range(12)], links_ref, clover_ref, halos)
    return [right_ref[m] - total[m] for m in range(12)]


def owner_table(blocks):
    places = lax.broadcasted_iota(jnp.int32, (blocks, LANES), 1)
    owners = places // (CZ * SPAN) * (CZ // SPAN) + places % CZ // SPAN
    return owners == lax.broadcasted_iota(jnp.int32, (blocks, LANES), 0)


def restrict_kernel(
    field_ref, right_ref, links_ref, clover_ref, t_back, t_ahead, x_back, x_ahead, null_ref, coarse_ref, summed_ref
):
    residual = residual_tiles(field_ref, right_ref, links_ref, clover_ref, t_back, t_ahead, x_back, x_ahead)
    rough = [r.astype(jnp.bfloat16).astype(jnp.float32) for r in residual]
    channels = summed_ref.shape[0]

    def one(k, _):
        total = None
        for m in range(12):
            term = null_ref[k * 12 + m].astype(jnp.float32) * rough[m]
            total = term if total is None else total + term
        summed_ref[pl.ds(k, 1), :] = jnp.sum(total, axis=0, keepdims=True)
        return 0

    lax.fori_loop(0, channels, one, 0, unroll=4)
    table = owner_table(coarse_ref.shape[0]).astype(jnp.float32)
    coarse_ref[...] = lax.dot_general(
        table, summed_ref[...], (((1,), (1,)), ((), ())), precision=exact_mode, preferred_element_type=jnp.float32
    )


def prolong_kernel(
    field_ref, links_ref, null_ref, approx_ref, updated_ref, t_up, t_down, x_up, x_down, spread_ref, work_ref
):
    channels, blocks = approx_ref.shape
    table = owner_table(blocks).astype(jnp.bfloat16)
    spread_ref[...] = jnp.dot(approx_ref[...].astype(jnp.bfloat16), table, preferred_element_type=jnp.float32)

    def one(k, totals):
        row = jnp.broadcast_to(spread_ref[pl.ds(k, 1), :], (ROWS, LANES))
        return tuple(totals[m] + null_ref[k * 12 + m].astype(jnp.float32) * row for m in range(12))

    start = tuple(jnp.zeros((ROWS, LANES), jnp.float32) for _ in range(12))
    added = lax.fori_loop(0, channels, one, start, unroll=4)
    updated = [field_ref[m] + added[m] for m in range(12)]
    for m in range(12):
        updated_ref[m] = updated[m]
    write_faces(updated, links_ref, (t_up, t_down, x_up, x_down), work_ref)


def residual_kernel(field_ref, right_ref, links_ref, clover_ref, t_back, t_ahead, x_back, x_ahead, out_ref):
    residual = residual_tiles(field_ref, right_ref, links_ref, clover_ref, t_back, t_ahead, x_back, x_ahead)
    for m in range(12):
        out_ref[m] = residual[m]


def call(kernel, outs, scratch, *args):
    return pl.pallas_call(
        kernel,
        out_shape=[jax.ShapeDtypeStruct(shape, jnp.float32) for shape in outs],
        in_specs=[VMEM] * len(args),
        out_specs=[VMEM] * len(outs),
        scratch_shapes=[pltpu.VMEM(shape, jnp.float32) for shape in scratch],
        compiler_params=pltpu.CompilerParams(vmem_limit_bytes=LIMIT),
    )(*args)


def moved(value, axis, step):
    size = lax.axis_size(axis)
    return lax.ppermute(value, axis, [(i, (i + step) % size) for i in range(size)])


def swap_faces(faces):
    t_up, t_down, x_up, x_down = faces
    return moved(t_up, "lat", 1), moved(t_down, "lat", -1), moved(x_up, "agg", 1), moved(x_down, "agg", -1)


def coarse_sweep(approx, coarse_rhs, inverse, couplings):
    grid = approx.reshape(CY // SPAN, CZ // SPAN, approx.shape[1])
    near = [moved(approx, "lat", -1), moved(approx, "lat", 1), moved(approx, "agg", -1), moved(approx, "agg", 1)]
    for axis in (0, 1):
        near.append(jnp.roll(grid, -1, axis).reshape(approx.shape))
        near.append(jnp.roll(grid, 1, axis).reshape(approx.shape))
    off_terms = jnp.einsum("dskl,dsl->sk", couplings, jnp.stack(near), precision=exact_mode)
    return jnp.einsum("skl,sl->sk", inverse, coarse_rhs - off_terms, precision=exact_mode)


def shards(solution, right_side, links, clover, null_vectors, coarse_inverse, coarse_links):
    shape = solution.shape
    tiles = (12, ROWS, LANES)
    field, right = solution.reshape(tiles), right_side.reshape(tiles)
    link_tiles = links.reshape(36, ROWS, LANES)
    clover_tiles = clover.reshape(72, ROWS, LANES)
    channels, blocks = coarse_inverse.shape[-1], coarse_inverse.shape[2]
    null_tiles = null_vectors.reshape(channels * 12, ROWS, LANES)
    inverse = coarse_inverse.astype(jnp.float32).reshape(blocks, channels, channels)
    couplings = coarse_links.astype(jnp.float32).reshape(8, blocks, channels, channels)
    face = (6 * FACE, LANES)

    halos = swap_faces(call(faces_kernel, [face] * 4, [tiles], field, link_tiles))
    (coarse_rhs,) = call(
        restrict_kernel,
        [(blocks, channels)],
        [(channels, LANES)],
        field,
        right,
        link_tiles,
        clover_tiles,
        *halos,
        null_tiles,
    )
    approx = jnp.einsum("skl,sl->sk", inverse, coarse_rhs, precision=exact_mode)
    for _ in range(SWEEPS):
        approx = coarse_sweep(approx, coarse_rhs, inverse, couplings)
    updated, *faces = call(
        prolong_kernel,
        [tiles] + [face] * 4,
        [(channels, LANES), tiles],
        field,
        link_tiles,
        null_tiles,
        approx.T,
    )
    halos = swap_faces(faces)
    (after,) = call(residual_kernel, [tiles], [], updated, right, link_tiles, clover_tiles, *halos)
    return updated.reshape(shape), after.reshape(shape)


def solution(mesh):
    placed = (
        P(None, "lat", "agg", None),
        P(None, "lat", "agg", None),
        P(None, None, None, "lat", "agg", None),
        P(None, None, None, "lat", "agg", None),
        P(None, None, "lat", "agg", None),
        P("lat", "agg", None, None, None),
        P(None, "lat", "agg", None, None, None),
    )
    return jax.shard_map(
        shards,
        mesh=mesh,
        in_specs=placed,
        out_specs=(P(None, "lat", "agg", None), P(None, "lat", "agg", None)),
        check_vma=False,
    )
```

```python
import jax
import jax.numpy as jnp
from jax import lax
from jax.experimental import pallas as pl
from jax.experimental.pallas import tpu as pltpu
from jax.sharding import PartitionSpec as P

CY = 8
CZ = 16
SWEEPS = 2
ROWS = 16
LANES = 128
FACE = 4
SPAN = 4

exact_mode = lax.Precision.HIGHEST
hopping = 0.5
wilson_mass = 4.0

VMEM = pl.BlockSpec(memory_space=pltpu.VMEM)
SMEM = pl.BlockSpec(memory_space=pltpu.SMEM)
HBM = pl.BlockSpec(memory_space=pltpu.HBM)
LIMIT = 24 * 1024 * 1024

EXPAND = {
    (0, 1): ((0, 0, 1), (1, 1, 1), (2, 0, -1), (3, 1, -1)),
    (0, -1): ((0, 0, 1), (1, 1, 1), (2, 0, 1), (3, 1, 1)),
    (1, 1): ((0, 0, 1), (3, 0, -1), (1, 1, 1), (2, 1, -1)),
    (1, -1): ((0, 0, 1), (3, 0, 1), (1, 1, 1), (2, 1, 1)),
    (2, 1): ((2, 0, 1), (3, 1, 1)),
    (2, -1): ((0, 0, 1), (1, 1, 1)),
    (3, 1): ((0, 0, 1), (1, 0, -1), (2, 1, 1), (3, 1, 1)),
    (3, -1): ((0, 0, 1), (1, 0, 1), (2, 1, 1), (3, 1, -1)),
}


def half(v, axis, direction):
    def mix(a, b, sign):
        return [v[a * 3 + c] + v[b * 3 + c] if sign > 0 else v[a * 3 + c] - v[b * 3 + c] for c in range(3)]

    if axis == 0:
        return mix(0, 2, -direction) + mix(1, 3, -direction)
    if axis == 1:
        return mix(0, 3, -direction) + mix(1, 2, -direction)
    if axis == 2:
        first = 2 if direction == 1 else 0
        return [2.0 * v[first * 3 + c] for c in range(6)]
    return mix(0, 1, -direction) + mix(2, 3, direction)


def transport(links_ref, axis, h, transposed):
    found = [None] * 6
    for i in range(3):
        for j in range(3):
            u = links_ref[axis * 9 + (j * 3 + i if transposed else i * 3 + j)].astype(jnp.float32)
            for spin in range(2):
                term = u * h[spin * 3 + j]
                at = spin * 3 + i
                found[at] = term if found[at] is None else found[at] + term
    return found


def place(dim):
    return lax.broadcasted_iota(jnp.int32, (ROWS, LANES), dim)


def edge_mask(axis, direction):
    rows = place(0)
    where = rows // FACE if axis == 0 else rows % FACE
    return where == (FACE - 1 if direction == 1 else 0)


def shifted(value, axis, direction):
    if axis < 2:
        moved = pltpu.roll(value, (-direction * (FACE if axis == 0 else 1)) % ROWS, 0)
        return jnp.where(edge_mask(axis, direction), 0.0, moved)
    if axis == 2:
        return pltpu.roll(value, (-direction * CZ) % LANES, 1)
    inside = pltpu.roll(value, (-direction) % LANES, 1)
    wrapped = pltpu.roll(value, (direction * (CZ - 1)) % LANES, 1)
    edge = CZ - 1 if direction == 1 else 0
    return jnp.where(place(1) % CZ == edge, wrapped, inside)


def halo_tile(face, axis, direction):
    if axis == 0:
        tile = jnp.concatenate([face] * (ROWS // FACE), axis=0)
    else:
        tile = jnp.broadcast_to(face[0:1], (ROWS, LANES))
        for t in range(1, FACE):
            tile = jnp.where(place(0) // FACE == t, jnp.broadcast_to(face[t : t + 1], (ROWS, LANES)), tile)
    return jnp.where(edge_mask(axis, direction), tile, 0.0)


def add_hop(hops, near, axis, direction):
    for spin, part, sign in EXPAND[axis, direction]:
        for c in range(3):
            at, term = spin * 3 + c, near[part * 3 + c]
            if hops[at] is None:
                hops[at] = term if sign > 0 else -term
            else:
                hops[at] = hops[at] + term if sign > 0 else hops[at] - term


def dirac_inside(v, links_ref, clover_ref):
    hops = [None] * 12
    for axis in range(4):
        for direction in (1, -1):
            h = half(v, axis, direction)
            if direction == -1:
                h = transport(links_ref, axis, h, True)
            near = []
            for c in range(6):
                near.append(shifted(h[c], axis, direction))
            if direction == 1:
                near = transport(links_ref, axis, near, False)
            add_hop(hops, near, axis, direction)
    total = []
    for block in range(2):
        for i in range(6):
            local = None
            for j in range(6):
                term = clover_ref[(block * 6 + i) * 6 + j].astype(jnp.float32) * v[block * 6 + j]
                local = term if local is None else local + term
            at = block * 6 + i
            total.append(wilson_mass * v[at] + local - hopping * hops[at])
    return total


def rows_of(c):
    return slice(c * FACE, (c + 1) * FACE)


def write_faces(v, links_ref, odd, faces, work_ref):
    t_first, t_second, x_up, x_down = faces
    back = transport(links_ref, 0, half(v, 0, -1), True)
    ahead = half(v, 0, 1)
    for c in range(6):
        up, down = back[c][ROWS - FACE :], ahead[c][:FACE]
        t_first[rows_of(c), :] = jnp.where(odd, down, up)
        t_second[rows_of(c), :] = jnp.where(odd, up, down)
    back = transport(links_ref, 1, half(v, 1, -1), True)
    ahead = half(v, 1, 1)
    for c in range(6):
        work_ref[c] = back[c]
        work_ref[6 + c] = ahead[c]
    for c in range(6):
        x_up[rows_of(c), :] = work_ref[c, pl.ds(FACE - 1, FACE, stride=FACE), :]
        x_down[rows_of(c), :] = work_ref[6 + c, pl.ds(0, FACE, stride=FACE), :]


def faces_kernel(odd_ref, field_hbm, links_hbm, field_ref, links_ref, t_first, t_second, x_up, x_down, work_ref, sems):
    copies = [
        pltpu.make_async_copy(field_hbm, field_ref, sems.at[0]),
        pltpu.make_async_copy(links_hbm, links_ref, sems.at[1]),
    ]
    for copy in copies:
        copy.start()
    for copy in copies:
        copy.wait()
    field = [field_ref[m] for m in range(12)]
    write_faces(field, links_ref, odd_ref[0] == 1, (t_first, t_second, x_up, x_down), work_ref)


def inside_first_kernel(
    field_ref, links_ref, right_hbm, clover_hbm, null_hbm, inside_ref, right_ref, clover_ref, null_ref, sems
):
    copies = [
        pltpu.make_async_copy(clover_hbm, clover_ref, sems.at[0]),
        pltpu.make_async_copy(right_hbm, right_ref, sems.at[1]),
        pltpu.make_async_copy(null_hbm, null_ref, sems.at[2]),
    ]
    for copy in copies:
        copy.start()
    copies[0].wait()
    copies[1].wait()
    total = dirac_inside([field_ref[m] for m in range(12)], links_ref, clover_ref)
    for m in range(12):
        inside_ref[m] = right_ref[m] - total[m]
    copies[2].wait()


def inside_kernel(field_ref, links_ref, right_ref, clover_ref, inside_ref, out_ref):
    field = [field_ref[m] for m in range(12)]
    total = dirac_inside(field, links_ref, clover_ref)
    for m in range(12):
        out_ref[m] = field[m]
        inside_ref[m] = right_ref[m] - total[m]


def residual_tiles(odd_ref, inside_ref, links_ref, x_back, x_ahead, t_first, t_second):
    odd = odd_ref[0] == 1
    hops = [None] * 12
    for axis in range(2):
        for direction in (1, -1):
            near = []
            for c in range(6):
                if axis == 1:
                    face = (x_ahead if direction == 1 else x_back)[rows_of(c), :]
                else:
                    first, second = t_first[rows_of(c), :], t_second[rows_of(c), :]
                    face = jnp.where(odd, second, first) if direction == 1 else jnp.where(odd, first, second)
                near.append(halo_tile(face, axis, direction))
            if direction == 1:
                near = transport(links_ref, axis, near, False)
            add_hop(hops, near, axis, direction)
    return [inside_ref[m] + hopping * hops[m] for m in range(12)]


def owner_table(blocks):
    places = lax.broadcasted_iota(jnp.int32, (blocks, LANES), 1)
    owners = places // (CZ * SPAN) * (CZ // SPAN) + places % CZ // SPAN
    return owners == lax.broadcasted_iota(jnp.int32, (blocks, LANES), 0)


def pieces(value, count):
    found = []
    for _ in range(count):
        part = value.astype(jnp.bfloat16)
        value = value - part.astype(jnp.float32)
        found.append(part)
    return found


def times_inverse(value, inverse_ref):
    blocks = value.shape[0]
    parts = pieces(value, 3)
    rows = []
    for s in range(blocks):
        total = None
        for part in parts:
            term = lax.dot_general(part, inverse_ref[s], (((1,), (1,)), ((), ())), preferred_element_type=jnp.float32)
            total = term if total is None else total + term
        rows.append(total[s : s + 1])
    return jnp.concatenate(rows, axis=0)


def sweep(odd, approx_ref, rhs_ref, near_refs, couplings_ref, inverse_ref):
    x_back, x_ahead, t_first, t_second = near_refs
    blocks, channels = approx_ref.shape
    first, second = t_first[...], t_second[...]
    ahead, back = jnp.where(odd, second, first), jnp.where(odd, first, second)
    mine, right, left = approx_ref[...], x_ahead[...], x_back[...]
    ones = jnp.ones((blocks, channels), jnp.bfloat16)
    deep = CZ // SPAN
    rows = []
    for s in range(blocks):
        other, z = (s + deep) % blocks, s // deep * deep
        up, down = z + (s + 1) % deep, z + (s - 1) % deep
        sources = (ahead, s), (back, s), (right, s), (left, s), (mine, other), (mine, other), (mine, up), (mine, down)
        total = None
        for d, (source, at) in enumerate(sources):
            row = jnp.broadcast_to(source[at : at + 1], (channels, channels))
            term = couplings_ref[d * blocks + s].astype(jnp.float32) * row
            total = term if total is None else total + term
        off = None
        for part in pieces(total, 2):
            term = lax.dot_general(ones, part, (((1,), (1,)), ((), ())), preferred_element_type=jnp.float32)
            off = term if off is None else off + term
        rows.append(off[s : s + 1])
    return times_inverse(rhs_ref[...] - jnp.concatenate(rows, axis=0), inverse_ref)


def sweep_kernel(
    odd_ref, approx_ref, rhs_ref, x_back, x_ahead, t_first, t_second, couplings_ref, inverse_ref, out_ref
):
    near = (x_back, x_ahead, t_first, t_second)
    out_ref[...] = sweep(odd_ref[0] == 1, approx_ref, rhs_ref, near, couplings_ref, inverse_ref)


def restrict_kernel(
    odd_ref, inside_ref, links_ref, x_back, x_ahead, t_first, t_second, null_ref, inverse_ref, coarse_ref, approx_ref, summed_ref
):
    residual = residual_tiles(odd_ref, inside_ref, links_ref, x_back, x_ahead, t_first, t_second)
    rough = [r.astype(jnp.bfloat16).astype(jnp.float32) for r in residual]
    channels = summed_ref.shape[0]

    def one(k, _):
        total = None
        for m in range(12):
            term = null_ref[k * 12 + m].astype(jnp.float32) * rough[m]
            total = term if total is None else total + term
        summed_ref[pl.ds(k, 1), :] = jnp.sum(total, axis=0, keepdims=True)
        return 0

    lax.fori_loop(0, channels, one, 0, unroll=4)
    table = owner_table(coarse_ref.shape[0]).astype(jnp.float32)
    coarse = lax.dot_general(
        table, summed_ref[...], (((1,), (1,)), ((), ())), precision=exact_mode, preferred_element_type=jnp.float32
    )
    coarse_ref[...] = coarse
    approx_ref[...] = times_inverse(coarse, inverse_ref)


def prolong_kernel(
    odd_ref,
    approx_ref,
    rhs_ref,
    x_back,
    x_ahead,
    t_back,
    t_ahead,
    couplings_ref,
    inverse_ref,
    field_ref,
    links_ref,
    null_ref,
    updated_ref,
    t_first,
    t_second,
    x_up,
    x_down,
    spread_ref,
    work_ref,
):
    blocks, channels = approx_ref.shape
    near = (x_back, x_ahead, t_back, t_ahead)
    approx = sweep(odd_ref[0] == 1, approx_ref, rhs_ref, near, couplings_ref, inverse_ref)
    table = owner_table(blocks).astype(jnp.bfloat16)
    spread_ref[...] = lax.dot_general(
        approx.astype(jnp.bfloat16), table, (((0,), (0,)), ((), ())), preferred_element_type=jnp.float32
    )

    def one(k, totals):
        row = jnp.broadcast_to(spread_ref[pl.ds(k, 1), :], (ROWS, LANES))
        return tuple(totals[m] + null_ref[k * 12 + m].astype(jnp.float32) * row for m in range(12))

    start = tuple(jnp.zeros((ROWS, LANES), jnp.float32) for _ in range(12))
    added = lax.fori_loop(0, channels, one, start, unroll=4)
    updated = [field_ref[m] + added[m] for m in range(12)]
    for m in range(12):
        updated_ref[m] = updated[m]
    write_faces(updated, links_ref, odd_ref[0] == 1, (t_first, t_second, x_up, x_down), work_ref)


def residual_kernel(odd_ref, inside_ref, links_ref, x_back, x_ahead, t_first, t_second, out_ref):
    residual = residual_tiles(odd_ref, inside_ref, links_ref, x_back, x_ahead, t_first, t_second)
    for m in range(12):
        out_ref[m] = residual[m]


def call(kernel, outs, scratch, *args, far=(), sems=0, cost=None):
    args = [pltpu.with_memory_space_constraint(arg, pltpu.HBM) if i in far else arg for i, arg in enumerate(args)]
    scratch_shapes = [pltpu.VMEM(shape, jnp.float32) for shape in scratch]
    if sems:
        scratch_shapes.append(pltpu.SemaphoreType.DMA((sems,)))
    return pl.pallas_call(
        kernel,
        out_shape=[jax.ShapeDtypeStruct(*out) for out in outs],
        in_specs=[SMEM if arg.dtype == jnp.int32 else HBM if i in far else VMEM for i, arg in enumerate(args)],
        out_specs=[VMEM] * len(outs),
        scratch_shapes=scratch_shapes,
        compiler_params=pltpu.CompilerParams(vmem_limit_bytes=LIMIT),
        cost_estimate=cost,
    )(*args)


def moved(value, axis, step):
    size = lax.axis_size(axis)
    return lax.ppermute(value, axis, [(i, (i + step) % size) for i in range(size)])


def traded(value, axis, second):
    size = lax.axis_size(axis)
    return lax.ppermute(value, axis, [(i, (i + (1 if i % 2 == second else -1)) % size) for i in range(size)])


def swapped(x_up, x_down, t_first, t_second):
    return moved(x_up, "agg", 1), moved(x_down, "agg", -1), traded(t_first, "lat", 0), traded(t_second, "lat", 1)


def shards(solution, right_side, links, clover, null_vectors, coarse_inverse, coarse_links):
    shape = solution.shape
    blocks, channels = coarse_inverse.shape[2], coarse_inverse.shape[-1]
    field = solution.reshape(12, ROWS, LANES)
    right = right_side.reshape(field.shape)
    link_tiles = links.reshape(36, ROWS, LANES)
    clover_tiles = clover.reshape(72, ROWS, LANES)
    null_tiles = null_vectors.reshape(channels * 12, ROWS, LANES)
    inverse = coarse_inverse.reshape(blocks, channels, channels)
    couplings = coarse_links.reshape(8 * blocks, channels, channels)

    tiles, face = (field.shape, jnp.float32), ((6 * FACE, LANES), jnp.float32)
    coarse = ((blocks, channels), jnp.float32)
    work, sums = field.shape, (channels, LANES)
    odd = (lax.axis_index("lat") % 2).astype(jnp.int32).reshape(1)
    beside = pl.CostEstimate(flops=4_000_000, bytes_accessed=6_000_000, transcendentals=0)

    def staged(array):
        return (array.shape, array.dtype)

    field, link_tiles, t_first, t_second, x_up, x_down = call(
        faces_kernel,
        [tiles, staged(link_tiles)] + [face] * 4,
        [work],
        odd,
        field,
        link_tiles,
        far=(1, 2),
        sems=2,
    )
    halos = swapped(x_up, x_down, t_first, t_second)
    inside, right, clover_tiles, null_tiles = call(
        inside_first_kernel,
        [tiles, tiles, staged(clover_tiles), staged(null_tiles)],
        [],
        field,
        link_tiles,
        right,
        clover_tiles,
        null_tiles,
        far=(2, 3, 4),
        sems=3,
        cost=beside,
    )
    rhs, approx = call(
        restrict_kernel, [coarse, coarse], [sums], odd, inside, link_tiles, *halos, null_tiles, inverse
    )
    for _ in range(SWEEPS - 1):
        near = swapped(approx, approx, approx, approx)
        (approx,) = call(sweep_kernel, [coarse], [], odd, approx, rhs, *near, couplings, inverse)
    near = swapped(approx, approx, approx, approx)
    updated, t_first, t_second, x_up, x_down = call(
        prolong_kernel,
        [tiles] + [face] * 4,
        [sums, work],
        odd,
        approx,
        rhs,
        *near,
        couplings,
        inverse,
        field,
        link_tiles,
        null_tiles,
    )
    halos = swapped(x_up, x_down, t_first, t_second)
    inside, updated = call(inside_kernel, [tiles, tiles], [], updated, link_tiles, right, clover_tiles, cost=beside)
    (after,) = call(residual_kernel, [tiles], [], odd, inside, link_tiles, *halos)
    return updated.reshape(shape), after.reshape(shape)


def solution(mesh):
    placed = (
        P(None, "lat", "agg", None),
        P(None, "lat", "agg", None),
        P(None, None, None, "lat", "agg", None),
        P(None, None, None, "lat", "agg", None),
        P(None, None, "lat", "agg", None),
        P("lat", "agg", None, None, None),
        P(None, "lat", "agg", None, None, None),
    )
    return jax.shard_map(
        shards,
        mesh=mesh,
        in_specs=placed,
        out_specs=(P(None, "lat", "agg", None), P(None, "lat", "agg", None)),
        check_vma=False,
    )
```

```python
import jax
import jax.numpy as jnp
from jax import lax
from jax.experimental import pallas as pl
from jax.experimental.pallas import tpu as pltpu
from jax.sharding import PartitionSpec as P

CY = 8
CZ = 16
SWEEPS = 2
ROWS = 16
LANES = 128
FACE = 4
SPAN = 4

exact_mode = lax.Precision.HIGHEST
hopping = 0.5
wilson_mass = 4.0

VMEM = pl.BlockSpec(memory_space=pltpu.VMEM)
SMEM = pl.BlockSpec(memory_space=pltpu.SMEM)
HBM = pl.BlockSpec(memory_space=pltpu.HBM)
LIMIT = 24 * 1024 * 1024

EXPAND = {
    (0, 1): ((0, 0, 1), (1, 1, 1), (2, 0, -1), (3, 1, -1)),
    (0, -1): ((0, 0, 1), (1, 1, 1), (2, 0, 1), (3, 1, 1)),
    (1, 1): ((0, 0, 1), (3, 0, -1), (1, 1, 1), (2, 1, -1)),
    (1, -1): ((0, 0, 1), (3, 0, 1), (1, 1, 1), (2, 1, 1)),
    (2, 1): ((2, 0, 1), (3, 1, 1)),
    (2, -1): ((0, 0, 1), (1, 1, 1)),
    (3, 1): ((0, 0, 1), (1, 0, -1), (2, 1, 1), (3, 1, 1)),
    (3, -1): ((0, 0, 1), (1, 0, 1), (2, 1, 1), (3, 1, -1)),
}


def half(v, axis, direction):
    def mix(a, b, sign):
        return [v[a * 3 + c] + v[b * 3 + c] if sign > 0 else v[a * 3 + c] - v[b * 3 + c] for c in range(3)]

    if axis == 0:
        return mix(0, 2, -direction) + mix(1, 3, -direction)
    if axis == 1:
        return mix(0, 3, -direction) + mix(1, 2, -direction)
    if axis == 2:
        first = 2 if direction == 1 else 0
        return [2.0 * v[first * 3 + c] for c in range(6)]
    return mix(0, 1, -direction) + mix(2, 3, direction)


def transport(links_ref, axis, h, transposed):
    found = [None] * 6
    for i in range(3):
        for j in range(3):
            u = links_ref[axis * 9 + (j * 3 + i if transposed else i * 3 + j)].astype(jnp.float32)
            for spin in range(2):
                term = u * h[spin * 3 + j]
                at = spin * 3 + i
                found[at] = term if found[at] is None else found[at] + term
    return found


def place(dim):
    return lax.broadcasted_iota(jnp.int32, (ROWS, LANES), dim)


def edge_mask(axis, direction):
    rows = place(0)
    where = rows // FACE if axis == 0 else rows % FACE
    return where == (FACE - 1 if direction == 1 else 0)


def shifted(value, axis, direction):
    if axis < 2:
        moved = pltpu.roll(value, (-direction * (FACE if axis == 0 else 1)) % ROWS, 0)
        return jnp.where(edge_mask(axis, direction), 0.0, moved)
    if axis == 2:
        return pltpu.roll(value, (-direction * CZ) % LANES, 1)
    inside = pltpu.roll(value, (-direction) % LANES, 1)
    wrapped = pltpu.roll(value, (direction * (CZ - 1)) % LANES, 1)
    edge = CZ - 1 if direction == 1 else 0
    return jnp.where(place(1) % CZ == edge, wrapped, inside)


def halo_tile(face, axis, direction):
    if axis == 0:
        tile = jnp.concatenate([face] * (ROWS // FACE), axis=0)
    else:
        tile = jnp.broadcast_to(face[0:1], (ROWS, LANES))
        for t in range(1, FACE):
            tile = jnp.where(place(0) // FACE == t, jnp.broadcast_to(face[t : t + 1], (ROWS, LANES)), tile)
    return jnp.where(edge_mask(axis, direction), tile, 0.0)


def add_hop(hops, near, axis, direction):
    for spin, part, sign in EXPAND[axis, direction]:
        for c in range(3):
            at, term = spin * 3 + c, near[part * 3 + c]
            if hops[at] is None:
                hops[at] = term if sign > 0 else -term
            else:
                hops[at] = hops[at] + term if sign > 0 else hops[at] - term


def dirac_inside(v, links_ref, clover_ref):
    hops = [None] * 12
    for axis in range(4):
        for direction in (1, -1):
            h = half(v, axis, direction)
            if direction == -1:
                h = transport(links_ref, axis, h, True)
            near = []
            for c in range(6):
                near.append(shifted(h[c], axis, direction))
            if direction == 1:
                near = transport(links_ref, axis, near, False)
            add_hop(hops, near, axis, direction)
    total = []
    for block in range(2):
        for i in range(6):
            local = None
            for j in range(6):
                term = clover_ref[(block * 6 + i) * 6 + j].astype(jnp.float32) * v[block * 6 + j]
                local = term if local is None else local + term
            at = block * 6 + i
            total.append(wilson_mass * v[at] + local - hopping * hops[at])
    return total


def rows_of(c):
    return slice(c * FACE, (c + 1) * FACE)


def write_faces(v, links_ref, odd, faces, work_ref):
    t_first, t_second, x_up, x_down = faces
    back = transport(links_ref, 0, half(v, 0, -1), True)
    ahead = half(v, 0, 1)
    for c in range(6):
        up, down = back[c][ROWS - FACE :], ahead[c][:FACE]
        t_first[rows_of(c), :] = jnp.where(odd, down, up)
        t_second[rows_of(c), :] = jnp.where(odd, up, down)
    back = transport(links_ref, 1, half(v, 1, -1), True)
    ahead = half(v, 1, 1)
    for c in range(6):
        work_ref[c] = back[c]
        work_ref[6 + c] = ahead[c]
    for c in range(6):
        x_up[rows_of(c), :] = work_ref[c, pl.ds(FACE - 1, FACE, stride=FACE), :]
        x_down[rows_of(c), :] = work_ref[6 + c, pl.ds(0, FACE, stride=FACE), :]


def faces_kernel(odd_ref, field_hbm, links_hbm, field_ref, links_ref, t_first, t_second, x_up, x_down, work_ref, sems):
    copies = [
        pltpu.make_async_copy(field_hbm, field_ref, sems.at[0]),
        pltpu.make_async_copy(links_hbm, links_ref, sems.at[1]),
    ]
    for copy in copies:
        copy.start()
    for copy in copies:
        copy.wait()
    field = [field_ref[m] for m in range(12)]
    write_faces(field, links_ref, odd_ref[0] == 1, (t_first, t_second, x_up, x_down), work_ref)


def inside_first_kernel(
    field_ref, links_ref, right_hbm, clover_hbm, null_hbm, inside_ref, right_ref, clover_ref, null_ref, sems
):
    copies = [
        pltpu.make_async_copy(clover_hbm, clover_ref, sems.at[0]),
        pltpu.make_async_copy(right_hbm, right_ref, sems.at[1]),
        pltpu.make_async_copy(null_hbm, null_ref, sems.at[2]),
    ]
    for copy in copies:
        copy.start()
    copies[0].wait()
    copies[1].wait()
    total = dirac_inside([field_ref[m] for m in range(12)], links_ref, clover_ref)
    for m in range(12):
        inside_ref[m] = right_ref[m] - total[m]
    copies[2].wait()


def inside_kernel(field_ref, links_ref, right_ref, clover_ref, inside_ref, out_ref):
    field = [field_ref[m] for m in range(12)]
    total = dirac_inside(field, links_ref, clover_ref)
    for m in range(12):
        out_ref[m] = field[m]
        inside_ref[m] = right_ref[m] - total[m]


def residual_tiles(odd_ref, inside_ref, links_ref, x_back, x_ahead, t_first, t_second):
    odd = odd_ref[0] == 1
    hops = [None] * 12
    for axis in range(2):
        for direction in (1, -1):
            near = []
            for c in range(6):
                if axis == 1:
                    face = (x_ahead if direction == 1 else x_back)[rows_of(c), :]
                else:
                    first, second = t_first[rows_of(c), :], t_second[rows_of(c), :]
                    face = jnp.where(odd, second, first) if direction == 1 else jnp.where(odd, first, second)
                near.append(halo_tile(face, axis, direction))
            if direction == 1:
                near = transport(links_ref, axis, near, False)
            add_hop(hops, near, axis, direction)
    return [inside_ref[m] + hopping * hops[m] for m in range(12)]


def owner_table(blocks):
    places = lax.broadcasted_iota(jnp.int32, (blocks, LANES), 1)
    owners = places // (CZ * SPAN) * (CZ // SPAN) + places % CZ // SPAN
    return owners == lax.broadcasted_iota(jnp.int32, (blocks, LANES), 0)


def pieces(value, count):
    found = []
    for _ in range(count):
        part = value.astype(jnp.bfloat16)
        value = value - part.astype(jnp.float32)
        found.append(part)
    return found


def times_inverse(value, inverse_ref):
    blocks = value.shape[0]
    parts = pieces(value, 3)
    rows = []
    for s in range(blocks):
        total = None
        for part in parts:
            term = lax.dot_general(part, inverse_ref[s], (((1,), (1,)), ((), ())), preferred_element_type=jnp.float32)
            total = term if total is None else total + term
        rows.append(total[s : s + 1])
    return jnp.concatenate(rows, axis=0)


def sweep(odd, approx_ref, rhs_ref, near_refs, couplings_ref, inverse_ref):
    x_back, x_ahead, t_first, t_second = near_refs
    blocks, channels = approx_ref.shape
    first, second = t_first[...], t_second[...]
    ahead, back = jnp.where(odd, second, first), jnp.where(odd, first, second)
    mine, right, left = approx_ref[...], x_ahead[...], x_back[...]
    ones = jnp.ones((blocks, channels), jnp.bfloat16)
    deep = CZ // SPAN
    rows = []
    for s in range(blocks):
        other, z = (s + deep) % blocks, s // deep * deep
        up, down = z + (s + 1) % deep, z + (s - 1) % deep
        sources = (ahead, s), (back, s), (right, s), (left, s), (mine, other), (mine, other), (mine, up), (mine, down)
        total = None
        for d, (source, at) in enumerate(sources):
            row = jnp.broadcast_to(source[at : at + 1], (channels, channels))
            term = couplings_ref[d * blocks + s].astype(jnp.float32) * row
            total = term if total is None else total + term
        off = None
        for part in pieces(total, 2):
            term = lax.dot_general(ones, part, (((1,), (1,)), ((), ())), preferred_element_type=jnp.float32)
            off = term if off is None else off + term
        rows.append(off[s : s + 1])
    return times_inverse(rhs_ref[...] - jnp.concatenate(rows, axis=0), inverse_ref)


def sweep_kernel(
    odd_ref, approx_ref, rhs_ref, x_back, x_ahead, t_first, t_second, couplings_ref, inverse_ref, out_ref
):
    near = (x_back, x_ahead, t_first, t_second)
    out_ref[...] = sweep(odd_ref[0] == 1, approx_ref, rhs_ref, near, couplings_ref, inverse_ref)


def restrict_kernel(
    odd_ref, inside_ref, links_ref, t_second, t_first, x_ahead, x_back, null_ref, inverse_ref, coarse_ref, approx_ref, summed_ref
):
    residual = residual_tiles(odd_ref, inside_ref, links_ref, x_back, x_ahead, t_first, t_second)
    rough = [r.astype(jnp.bfloat16).astype(jnp.float32) for r in residual]
    channels = summed_ref.shape[0]

    def one(k, _):
        total = None
        for m in range(12):
            term = null_ref[k * 12 + m].astype(jnp.float32) * rough[m]
            total = term if total is None else total + term
        summed_ref[pl.ds(k, 1), :] = jnp.sum(total, axis=0, keepdims=True)
        return 0

    lax.fori_loop(0, channels, one, 0, unroll=4)
    table = owner_table(coarse_ref.shape[0]).astype(jnp.float32)
    coarse = lax.dot_general(
        table, summed_ref[...], (((1,), (1,)), ((), ())), precision=exact_mode, preferred_element_type=jnp.float32
    )
    coarse_ref[...] = coarse
    approx_ref[...] = times_inverse(coarse, inverse_ref)


def prolong_kernel(
    odd_ref,
    approx_ref,
    rhs_ref,
    x_back,
    x_ahead,
    t_back,
    t_ahead,
    couplings_ref,
    inverse_ref,
    field_ref,
    links_ref,
    null_ref,
    updated_ref,
    t_first,
    t_second,
    x_up,
    x_down,
    spread_ref,
    work_ref,
):
    blocks, channels = approx_ref.shape
    near = (x_back, x_ahead, t_back, t_ahead)
    approx = sweep(odd_ref[0] == 1, approx_ref, rhs_ref, near, couplings_ref, inverse_ref)
    table = owner_table(blocks).astype(jnp.bfloat16)
    spread_ref[...] = lax.dot_general(
        approx.astype(jnp.bfloat16), table, (((0,), (0,)), ((), ())), preferred_element_type=jnp.float32
    )

    def one(k, totals):
        row = jnp.broadcast_to(spread_ref[pl.ds(k, 1), :], (ROWS, LANES))
        return tuple(totals[m] + null_ref[k * 12 + m].astype(jnp.float32) * row for m in range(12))

    start = tuple(jnp.zeros((ROWS, LANES), jnp.float32) for _ in range(12))
    added = lax.fori_loop(0, channels, one, start, unroll=4)
    updated = [field_ref[m] + added[m] for m in range(12)]
    for m in range(12):
        updated_ref[m] = updated[m]
    write_faces(updated, links_ref, odd_ref[0] == 1, (t_first, t_second, x_up, x_down), work_ref)


def residual_kernel(odd_ref, inside_ref, links_ref, t_second, t_first, x_ahead, x_back, out_ref):
    residual = residual_tiles(odd_ref, inside_ref, links_ref, x_back, x_ahead, t_first, t_second)
    for m in range(12):
        out_ref[m] = residual[m]


def call(kernel, outs, scratch, *args, far=(), sems=0, cost=None):
    args = [pltpu.with_memory_space_constraint(arg, pltpu.HBM) if i in far else arg for i, arg in enumerate(args)]
    scratch_shapes = [pltpu.VMEM(shape, jnp.float32) for shape in scratch]
    if sems:
        scratch_shapes.append(pltpu.SemaphoreType.DMA((sems,)))
    return pl.pallas_call(
        kernel,
        out_shape=[jax.ShapeDtypeStruct(*out) for out in outs],
        in_specs=[SMEM if arg.dtype == jnp.int32 else HBM if i in far else VMEM for i, arg in enumerate(args)],
        out_specs=[VMEM] * len(outs),
        scratch_shapes=scratch_shapes,
        compiler_params=pltpu.CompilerParams(vmem_limit_bytes=LIMIT),
        cost_estimate=cost,
    )(*args)


def moved(value, axis, step):
    size = lax.axis_size(axis)
    return lax.ppermute(value, axis, [(i, (i + step) % size) for i in range(size)])


def traded(value, axis, second):
    size = lax.axis_size(axis)
    return lax.ppermute(value, axis, [(i, (i + (1 if i % 2 == second else -1)) % size) for i in range(size)])


def swapped(x_up, x_down, t_first, t_second):
    return moved(x_up, "agg", 1), moved(x_down, "agg", -1), traded(t_first, "lat", 0), traded(t_second, "lat", 1)


def shards(solution, right_side, links, clover, null_vectors, coarse_inverse, coarse_links):
    shape = solution.shape
    blocks, channels = coarse_inverse.shape[2], coarse_inverse.shape[-1]
    field = solution.reshape(12, ROWS, LANES)
    right = right_side.reshape(field.shape)
    link_tiles = links.reshape(36, ROWS, LANES)
    clover_tiles = clover.reshape(72, ROWS, LANES)
    null_tiles = null_vectors.reshape(channels * 12, ROWS, LANES)
    inverse = coarse_inverse.reshape(blocks, channels, channels)
    couplings = coarse_links.reshape(8 * blocks, channels, channels)

    tiles, face = (field.shape, jnp.float32), ((6 * FACE, LANES), jnp.float32)
    coarse = ((blocks, channels), jnp.float32)
    work, sums = field.shape, (channels, LANES)
    odd = (lax.axis_index("lat") % 2).astype(jnp.int32).reshape(1)
    beside = pl.CostEstimate(flops=4_000_000, bytes_accessed=6_000_000, transcendentals=0)

    def staged(array):
        return (array.shape, array.dtype)

    field, link_tiles, t_first, t_second, x_up, x_down = call(
        faces_kernel,
        [tiles, staged(link_tiles)] + [face] * 4,
        [work],
        odd,
        field,
        link_tiles,
        far=(1, 2),
        sems=2,
    )
    halos = swapped(x_up, x_down, t_first, t_second)
    inside, right, clover_tiles, null_tiles = call(
        inside_first_kernel,
        [tiles, tiles, staged(clover_tiles), staged(null_tiles)],
        [],
        field,
        link_tiles,
        right,
        clover_tiles,
        null_tiles,
        far=(2, 3, 4),
        sems=3,
        cost=beside,
    )
    rhs, approx = call(
        restrict_kernel, [coarse, coarse], [sums], odd, inside, link_tiles, *halos[::-1], null_tiles, inverse
    )
    for _ in range(SWEEPS - 1):
        near = swapped(approx, approx, approx, approx)
        (approx,) = call(sweep_kernel, [coarse], [], odd, approx, rhs, *near, couplings, inverse)
    near = swapped(approx, approx, approx, approx)
    updated, t_first, t_second, x_up, x_down = call(
        prolong_kernel,
        [tiles] + [face] * 4,
        [sums, work],
        odd,
        approx,
        rhs,
        *near,
        couplings,
        inverse,
        field,
        link_tiles,
        null_tiles,
    )
    halos = swapped(x_up, x_down, t_first, t_second)
    inside, updated = call(inside_kernel, [tiles, tiles], [], updated, link_tiles, right, clover_tiles, cost=beside)
    (after,) = call(residual_kernel, [tiles], [], odd, inside, link_tiles, *halos[::-1])
    return updated.reshape(shape), after.reshape(shape)


def solution(mesh):
    placed = (
        P(None, "lat", "agg", None),
        P(None, "lat", "agg", None),
        P(None, None, None, "lat", "agg", None),
        P(None, None, None, "lat", "agg", None),
        P(None, None, "lat", "agg", None),
        P("lat", "agg", None, None, None),
        P(None, "lat", "agg", None, None, None),
    )
    return jax.shard_map(
        shards,
        mesh=mesh,
        in_specs=placed,
        out_specs=(P(None, "lat", "agg", None), P(None, "lat", "agg", None)),
        check_vma=False,
    )
```

```python
import jax
import jax.numpy as jnp
from jax import lax
from jax.experimental import pallas as pl
from jax.experimental.pallas import tpu as pltpu
from jax.sharding import PartitionSpec as P

CY = 8
CZ = 16
SWEEPS = 2
ROWS = 16
LANES = 128
FACE = 4
SPAN = 4

exact_mode = lax.Precision.HIGHEST
hopping = 0.5
wilson_mass = 4.0

VMEM = pl.BlockSpec(memory_space=pltpu.VMEM)
SMEM = pl.BlockSpec(memory_space=pltpu.SMEM)
HBM = pl.BlockSpec(memory_space=pltpu.HBM)
LIMIT = 24 * 1024 * 1024

EXPAND = {
    (0, 1): ((0, 0, 1), (1, 1, 1), (2, 0, -1), (3, 1, -1)),
    (0, -1): ((0, 0, 1), (1, 1, 1), (2, 0, 1), (3, 1, 1)),
    (1, 1): ((0, 0, 1), (3, 0, -1), (1, 1, 1), (2, 1, -1)),
    (1, -1): ((0, 0, 1), (3, 0, 1), (1, 1, 1), (2, 1, 1)),
    (2, 1): ((2, 0, 1), (3, 1, 1)),
    (2, -1): ((0, 0, 1), (1, 1, 1)),
    (3, 1): ((0, 0, 1), (1, 0, -1), (2, 1, 1), (3, 1, 1)),
    (3, -1): ((0, 0, 1), (1, 0, 1), (2, 1, 1), (3, 1, -1)),
}


def half(v, axis, direction):
    def mix(a, b, sign):
        return [v[a * 3 + c] + v[b * 3 + c] if sign > 0 else v[a * 3 + c] - v[b * 3 + c] for c in range(3)]

    if axis == 0:
        return mix(0, 2, -direction) + mix(1, 3, -direction)
    if axis == 1:
        return mix(0, 3, -direction) + mix(1, 2, -direction)
    if axis == 2:
        first = 2 if direction == 1 else 0
        return [2.0 * v[first * 3 + c] for c in range(6)]
    return mix(0, 1, -direction) + mix(2, 3, direction)


def transport(links_ref, axis, h, transposed):
    found = [None] * 6
    for i in range(3):
        for j in range(3):
            u = links_ref[axis * 9 + (j * 3 + i if transposed else i * 3 + j)].astype(jnp.float32)
            for spin in range(2):
                term = u * h[spin * 3 + j]
                at = spin * 3 + i
                found[at] = term if found[at] is None else found[at] + term
    return found


def place(dim):
    return lax.broadcasted_iota(jnp.int32, (ROWS, LANES), dim)


def edge_mask(axis, direction):
    rows = place(0)
    where = rows // FACE if axis == 0 else rows % FACE
    return where == (FACE - 1 if direction == 1 else 0)


def shifted(value, axis, direction):
    if axis < 2:
        moved = pltpu.roll(value, (-direction * (FACE if axis == 0 else 1)) % ROWS, 0)
        return jnp.where(edge_mask(axis, direction), 0.0, moved)
    if axis == 2:
        return pltpu.roll(value, (-direction * CZ) % LANES, 1)
    inside = pltpu.roll(value, (-direction) % LANES, 1)
    wrapped = pltpu.roll(value, (direction * (CZ - 1)) % LANES, 1)
    edge = CZ - 1 if direction == 1 else 0
    return jnp.where(place(1) % CZ == edge, wrapped, inside)


def halo_tile(face, axis, direction):
    if axis == 0:
        tile = jnp.concatenate([face] * (ROWS // FACE), axis=0)
    else:
        tile = jnp.broadcast_to(face[0:1], (ROWS, LANES))
        for t in range(1, FACE):
            tile = jnp.where(place(0) // FACE == t, jnp.broadcast_to(face[t : t + 1], (ROWS, LANES)), tile)
    return jnp.where(edge_mask(axis, direction), tile, 0.0)


def add_hop(hops, near, axis, direction):
    for spin, part, sign in EXPAND[axis, direction]:
        for c in range(3):
            at, term = spin * 3 + c, near[part * 3 + c]
            if hops[at] is None:
                hops[at] = term if sign > 0 else -term
            else:
                hops[at] = hops[at] + term if sign > 0 else hops[at] - term


def dirac_inside(v, links_ref, clover_ref):
    hops = [None] * 12
    for axis in range(4):
        for direction in (1, -1):
            h = half(v, axis, direction)
            if direction == -1:
                h = transport(links_ref, axis, h, True)
            near = []
            for c in range(6):
                near.append(shifted(h[c], axis, direction))
            if direction == 1:
                near = transport(links_ref, axis, near, False)
            add_hop(hops, near, axis, direction)
    total = []
    for block in range(2):
        for i in range(6):
            local = None
            for j in range(6):
                term = clover_ref[(block * 6 + i) * 6 + j].astype(jnp.float32) * v[block * 6 + j]
                local = term if local is None else local + term
            at = block * 6 + i
            total.append(wilson_mass * v[at] + local - hopping * hops[at])
    return total


def rows_of(c):
    return slice(c * FACE, (c + 1) * FACE)


def write_faces(v, links_ref, odd, faces, work_ref):
    t_first, t_second, x_up, x_down = faces
    back = transport(links_ref, 0, half(v, 0, -1), True)
    ahead = half(v, 0, 1)
    for c in range(6):
        up, down = back[c][ROWS - FACE :], ahead[c][:FACE]
        t_first[rows_of(c), :] = jnp.where(odd, down, up)
        t_second[rows_of(c), :] = jnp.where(odd, up, down)
    back = transport(links_ref, 1, half(v, 1, -1), True)
    ahead = half(v, 1, 1)
    for c in range(6):
        work_ref[c] = back[c]
        work_ref[6 + c] = ahead[c]
    for c in range(6):
        x_up[rows_of(c), :] = work_ref[c, pl.ds(FACE - 1, FACE, stride=FACE), :]
        x_down[rows_of(c), :] = work_ref[6 + c, pl.ds(0, FACE, stride=FACE), :]


def faces_kernel(odd_ref, field_hbm, links_hbm, field_ref, links_ref, t_first, t_second, x_up, x_down, work_ref, sems):
    copies = [
        pltpu.make_async_copy(field_hbm, field_ref, sems.at[0]),
        pltpu.make_async_copy(links_hbm, links_ref, sems.at[1]),
    ]
    for copy in copies:
        copy.start()
    for copy in copies:
        copy.wait()
    field = [field_ref[m] for m in range(12)]
    write_faces(field, links_ref, odd_ref[0] == 1, (t_first, t_second, x_up, x_down), work_ref)


def inside_first_kernel(
    field_ref, links_ref, right_hbm, clover_hbm, null_hbm, inside_ref, right_ref, clover_ref, null_ref, sems
):
    copies = [
        pltpu.make_async_copy(clover_hbm, clover_ref, sems.at[0]),
        pltpu.make_async_copy(right_hbm, right_ref, sems.at[1]),
        pltpu.make_async_copy(null_hbm, null_ref, sems.at[2]),
    ]
    for copy in copies:
        copy.start()
    copies[0].wait()
    copies[1].wait()
    total = dirac_inside([field_ref[m] for m in range(12)], links_ref, clover_ref)
    for m in range(12):
        inside_ref[m] = right_ref[m] - total[m]
    copies[2].wait()


def inside_kernel(field_ref, links_ref, right_ref, clover_ref, inside_ref, out_ref):
    field = [field_ref[m] for m in range(12)]
    total = dirac_inside(field, links_ref, clover_ref)
    for m in range(12):
        out_ref[m] = field[m]
        inside_ref[m] = right_ref[m] - total[m]


def residual_tiles(odd_ref, inside_ref, links_ref, x_back, x_ahead, t_first, t_second):
    odd = odd_ref[0] == 1
    hops = [None] * 12
    for axis in range(2):
        for direction in (1, -1):
            near = []
            for c in range(6):
                if axis == 1:
                    face = (x_ahead if direction == 1 else x_back)[rows_of(c), :]
                else:
                    first, second = t_first[rows_of(c), :], t_second[rows_of(c), :]
                    face = jnp.where(odd, second, first) if direction == 1 else jnp.where(odd, first, second)
                near.append(halo_tile(face, axis, direction))
            if direction == 1:
                near = transport(links_ref, axis, near, False)
            add_hop(hops, near, axis, direction)
    return [inside_ref[m] + hopping * hops[m] for m in range(12)]


def owner_table(blocks):
    places = lax.broadcasted_iota(jnp.int32, (blocks, LANES), 1)
    owners = places // (CZ * SPAN) * (CZ // SPAN) + places % CZ // SPAN
    return owners == lax.broadcasted_iota(jnp.int32, (blocks, LANES), 0)


def pieces(value, count):
    found = []
    for _ in range(count):
        part = value.astype(jnp.bfloat16)
        value = value - part.astype(jnp.float32)
        found.append(part)
    return found


def times_inverse(value, inverse_ref):
    blocks = value.shape[0]
    parts = pieces(value, 3)
    rows = []
    for s in range(blocks):
        total = None
        for part in parts:
            term = lax.dot_general(part, inverse_ref[s], (((1,), (1,)), ((), ())), preferred_element_type=jnp.float32)
            total = term if total is None else total + term
        rows.append(total[s : s + 1])
    return jnp.concatenate(rows, axis=0)


def sweep(odd, approx_ref, rhs_ref, near_refs, couplings_ref, inverse_ref):
    x_back, x_ahead, t_first, t_second = near_refs
    blocks, channels = approx_ref.shape
    first, second = t_first[...], t_second[...]
    ahead, back = jnp.where(odd, second, first), jnp.where(odd, first, second)
    mine, right, left = approx_ref[...], x_ahead[...], x_back[...]
    ones = jnp.ones((blocks, channels), jnp.bfloat16)
    deep = CZ // SPAN
    rows = []
    for s in range(blocks):
        other, z = (s + deep) % blocks, s // deep * deep
        up, down = z + (s + 1) % deep, z + (s - 1) % deep
        sources = (ahead, s), (back, s), (right, s), (left, s), (mine, other), (mine, other), (mine, up), (mine, down)
        total = None
        for d, (source, at) in enumerate(sources):
            row = jnp.broadcast_to(source[at : at + 1], (channels, channels))
            term = couplings_ref[d * blocks + s].astype(jnp.float32) * row
            total = term if total is None else total + term
        off = None
        for part in pieces(total, 2):
            term = lax.dot_general(ones, part, (((1,), (1,)), ((), ())), preferred_element_type=jnp.float32)
            off = term if off is None else off + term
        rows.append(off[s : s + 1])
    return times_inverse(rhs_ref[...] - jnp.concatenate(rows, axis=0), inverse_ref)


def sweep_kernel(
    odd_ref, approx_ref, rhs_ref, t_first, x_back, x_ahead, t_second, couplings_ref, inverse_ref, out_ref
):
    near = (x_back, x_ahead, t_first, t_second)
    out_ref[...] = sweep(odd_ref[0] == 1, approx_ref, rhs_ref, near, couplings_ref, inverse_ref)


def restrict_kernel(
    odd_ref, inside_ref, links_ref, t_second, x_ahead, x_back, t_first, null_ref, inverse_ref, coarse_ref, approx_ref, summed_ref
):
    residual = residual_tiles(odd_ref, inside_ref, links_ref, x_back, x_ahead, t_first, t_second)
    rough = [r.astype(jnp.bfloat16).astype(jnp.float32) for r in residual]
    channels = summed_ref.shape[0]

    def one(k, _):
        total = None
        for m in range(12):
            term = null_ref[k * 12 + m].astype(jnp.float32) * rough[m]
            total = term if total is None else total + term
        summed_ref[pl.ds(k, 1), :] = jnp.sum(total, axis=0, keepdims=True)
        return 0

    lax.fori_loop(0, channels, one, 0, unroll=4)
    table = owner_table(coarse_ref.shape[0]).astype(jnp.float32)
    coarse = lax.dot_general(
        table, summed_ref[...], (((1,), (1,)), ((), ())), precision=exact_mode, preferred_element_type=jnp.float32
    )
    coarse_ref[...] = coarse
    approx_ref[...] = times_inverse(coarse, inverse_ref)


def prolong_kernel(
    odd_ref,
    approx_ref,
    rhs_ref,
    t_back,
    x_back,
    x_ahead,
    t_ahead,
    couplings_ref,
    inverse_ref,
    field_ref,
    links_ref,
    null_ref,
    updated_ref,
    t_first,
    t_second,
    x_up,
    x_down,
    spread_ref,
    work_ref,
):
    blocks, channels = approx_ref.shape
    near = (x_back, x_ahead, t_back, t_ahead)
    approx = sweep(odd_ref[0] == 1, approx_ref, rhs_ref, near, couplings_ref, inverse_ref)
    table = owner_table(blocks).astype(jnp.bfloat16)
    spread_ref[...] = lax.dot_general(
        approx.astype(jnp.bfloat16), table, (((0,), (0,)), ((), ())), preferred_element_type=jnp.float32
    )

    def one(k, totals):
        row = jnp.broadcast_to(spread_ref[pl.ds(k, 1), :], (ROWS, LANES))
        return tuple(totals[m] + null_ref[k * 12 + m].astype(jnp.float32) * row for m in range(12))

    start = tuple(jnp.zeros((ROWS, LANES), jnp.float32) for _ in range(12))
    added = lax.fori_loop(0, channels, one, start, unroll=4)
    updated = [field_ref[m] + added[m] for m in range(12)]
    for m in range(12):
        updated_ref[m] = updated[m]
    write_faces(updated, links_ref, odd_ref[0] == 1, (t_first, t_second, x_up, x_down), work_ref)


def residual_kernel(odd_ref, inside_ref, links_ref, t_second, x_ahead, x_back, t_first, out_ref):
    residual = residual_tiles(odd_ref, inside_ref, links_ref, x_back, x_ahead, t_first, t_second)
    for m in range(12):
        out_ref[m] = residual[m]


def call(kernel, outs, scratch, *args, far=(), sems=0, cost=None):
    args = [pltpu.with_memory_space_constraint(arg, pltpu.HBM) if i in far else arg for i, arg in enumerate(args)]
    scratch_shapes = [pltpu.VMEM(shape, jnp.float32) for shape in scratch]
    if sems:
        scratch_shapes.append(pltpu.SemaphoreType.DMA((sems,)))
    return pl.pallas_call(
        kernel,
        out_shape=[jax.ShapeDtypeStruct(*out) for out in outs],
        in_specs=[SMEM if arg.dtype == jnp.int32 else HBM if i in far else VMEM for i, arg in enumerate(args)],
        out_specs=[VMEM] * len(outs),
        scratch_shapes=scratch_shapes,
        compiler_params=pltpu.CompilerParams(vmem_limit_bytes=LIMIT),
        cost_estimate=cost,
    )(*args)


def moved(value, axis, step):
    size = lax.axis_size(axis)
    return lax.ppermute(value, axis, [(i, (i + step) % size) for i in range(size)])


def traded(value, axis, second):
    size = lax.axis_size(axis)
    return lax.ppermute(value, axis, [(i, (i + (1 if i % 2 == second else -1)) % size) for i in range(size)])


def swapped(x_up, x_down, t_first, t_second):
    return moved(x_up, "agg", 1), moved(x_down, "agg", -1), traded(t_first, "lat", 0), traded(t_second, "lat", 1)


def by_start(x_back, x_ahead, t_first, t_second):
    return t_second, x_ahead, x_back, t_first


def shards(solution, right_side, links, clover, null_vectors, coarse_inverse, coarse_links):
    shape = solution.shape
    blocks, channels = coarse_inverse.shape[2], coarse_inverse.shape[-1]
    field = solution.reshape(12, ROWS, LANES)
    right = right_side.reshape(field.shape)
    link_tiles = links.reshape(36, ROWS, LANES)
    clover_tiles = clover.reshape(72, ROWS, LANES)
    null_tiles = null_vectors.reshape(channels * 12, ROWS, LANES)
    inverse = coarse_inverse.reshape(blocks, channels, channels)
    couplings = coarse_links.reshape(8 * blocks, channels, channels)

    tiles, face = (field.shape, jnp.float32), ((6 * FACE, LANES), jnp.float32)
    coarse = ((blocks, channels), jnp.float32)
    work, sums = field.shape, (channels, LANES)
    odd = (lax.axis_index("lat") % 2).astype(jnp.int32).reshape(1)
    beside = pl.CostEstimate(flops=4_000_000, bytes_accessed=6_000_000, transcendentals=0)

    def staged(array):
        return (array.shape, array.dtype)

    field, link_tiles, t_first, t_second, x_up, x_down = call(
        faces_kernel,
        [tiles, staged(link_tiles)] + [face] * 4,
        [work],
        odd,
        field,
        link_tiles,
        far=(1, 2),
        sems=2,
    )
    halos = swapped(x_up, x_down, t_first, t_second)
    inside, right, clover_tiles, null_tiles = call(
        inside_first_kernel,
        [tiles, tiles, staged(clover_tiles), staged(null_tiles)],
        [],
        field,
        link_tiles,
        right,
        clover_tiles,
        null_tiles,
        far=(2, 3, 4),
        sems=3,
        cost=beside,
    )
    rhs, approx = call(
        restrict_kernel, [coarse, coarse], [sums], odd, inside, link_tiles, *by_start(*halos), null_tiles, inverse
    )
    for _ in range(SWEEPS - 1):
        near = swapped(approx, approx, approx, approx)
        (approx,) = call(sweep_kernel, [coarse], [], odd, approx, rhs, *by_start(*near)[::-1], couplings, inverse)
    near = swapped(approx, approx, approx, approx)
    updated, t_first, t_second, x_up, x_down = call(
        prolong_kernel,
        [tiles] + [face] * 4,
        [sums, work],
        odd,
        approx,
        rhs,
        *by_start(*near)[::-1],
        couplings,
        inverse,
        field,
        link_tiles,
        null_tiles,
    )
    halos = swapped(x_up, x_down, t_first, t_second)
    inside, updated = call(inside_kernel, [tiles, tiles], [], updated, link_tiles, right, clover_tiles, cost=beside)
    (after,) = call(residual_kernel, [tiles], [], odd, inside, link_tiles, *by_start(*halos))
    return updated.reshape(shape), after.reshape(shape)


def solution(mesh):
    placed = (
        P(None, "lat", "agg", None),
        P(None, "lat", "agg", None),
        P(None, None, None, "lat", "agg", None),
        P(None, None, None, "lat", "agg", None),
        P(None, None, "lat", "agg", None),
        P("lat", "agg", None, None, None),
        P(None, "lat", "agg", None, None, None),
    )
    return jax.shard_map(
        shards,
        mesh=mesh,
        in_specs=placed,
        out_specs=(P(None, "lat", "agg", None), P(None, "lat", "agg", None)),
        check_vma=False,
    )
```
